32 devices in a mesh: groups: 2 (over y), wide: 4 (over z), narrow: 4 (over x, core).
Axes of the slice: x: 2, y: 2, z: 4, core: 2. Of those that a mesh axis runs over, the one named last changes fastest.
Arguments:
- tokens: bfloat16 [1024, 7168], P('groups', ('narrow', 'wide')), parts along dimension 0, may hold values from -6 to 6
- gate_one: bfloat16 [7168, 9216], P('narrow', 'wide'), may hold values from -0.0625 to 0.0625
- up_one: bfloat16 [7168, 9216], P('narrow', 'wide'), may hold values from -0.0625 to 0.0625
- down_one: bfloat16 [9216, 7168], P('wide', 'narrow'), may hold values from -0.09375 to 0.09375
- gate_two: bfloat16 [4, 1792, 9216], P(None, 'wide', 'narrow'), may hold values from -0.0625 to 0.0625
- up_two: bfloat16 [4, 1792, 9216], P(None, 'wide', 'narrow'), may hold values from -0.0625 to 0.0625
- down_two: bfloat16 [9216, 4, 1792], P('narrow', None, 'wide'), may hold values from -0.09375 to 0.09375
Outputs:
- result: bfloat16 [1024, 7168], P('groups', ('narrow', 'wide')), parts along dimension 0
The draws below stay inside these ranges and needn't reach their ends.
There are 2 independent parts, one for each index of `groups`. The reference program is written for one: setup_inputs(seed, part) draws one part's arguments, and reference() takes and returns one part's arrays. A program takes and returns all parts, laid end to end along the dimension named above; an argument that names none is the same for every part. Nothing has to cross between parts.
All inputs are finite; a program needn't handle non-finite values.
Results may differ from the reference program's by a relative error of at most 0.03.
Values may be sent and summed in bfloat16 or wider, within the bound.
A program may use at most 128 MiB of HBM per device.

```python
import jax
import jax.numpy as jnp
from jax import lax

H = 7168
F = 9216
TOKENS = 512
HB = 4
HC = 1792
N_WIDE = 4
N_NARROW = 4


def raised(entries, key, source, target, shards_of, factor):
    def block_of(dim):
        return (jnp.arange(entries.shape[dim]) // (entries.shape[dim] // shards_of)).reshape((-1,) + (1,) * (entries.ndim - 1 - dim))

    near = jax.random.permutation(key, shards_of)[block_of(target)]
    far = (block_of(target) + shards_of // 2) % shards_of
    return jnp.where((block_of(source) == near) | (block_of(source) == far), factor * entries, entries)


def levels(own_key, extent, pieces, least, largest):
    loudness = 1.0
    for dim, shards_of in pieces:
        draws = jax.random.uniform(jax.random.fold_in(jax.random.fold_in(own_key, 6), dim), (shards_of,), jnp.float32, least / len(pieces), largest / len(pieces))
        loudness = loudness * jnp.repeat(jnp.exp(draws), extent[dim] // shards_of).reshape((-1,) + (1,) * (len(extent) - 1 - dim))
    return loudness


def bell_draw(rng, shape, width, bound, cuts=(), kind=jnp.bfloat16):
    array = width * jax.random.normal(rng, shape, jnp.float32)
    if cuts:
        array = array * levels(rng, shape, cuts, -0.22, 0.18)
    return jnp.clip(array, -bound, bound).astype(kind)


def noise_with(own_key, extent, width, bound, pieces, heavy, dtype=jnp.bfloat16):
    result = width * jax.random.normal(own_key, extent, jnp.float32)
    if pieces:
        result = result * levels(own_key, extent, pieces, -0.22, 0.18)
    return jnp.clip(raised(result, jax.random.fold_in(own_key, 3), *heavy), -bound, bound).astype(dtype)


def setup_inputs(seed: int = 0, part: int = 0) -> dict:
    key_of = jax.random.split(jax.random.key(seed), 8)
    own_keys = jax.random.split(jax.random.fold_in(key_of[7], part), 8)
    tokens = bell_draw(own_keys[0], (TOKENS, H), 1.0, 6.0, ((1, 16),))
    gate_one = bell_draw(key_of[1], (H, F), H ** -0.5, 0.0625, ((0, 4), (1, 4)))
    up_one = bell_draw(key_of[2], (H, F), H ** -0.5, 0.0625, ((0, 4), (1, 4)))
    down_one = noise_with(key_of[3], (F, H), F ** -0.5, 0.09375, ((0, 4), (1, 4)), (0, 1, 4, 2.0))
    gate_two = bell_draw(key_of[4], (HB, HC, F), H ** -0.5, 0.0625, ((1, 4), (2, 4)))
    up_two = bell_draw(key_of[5], (HB, HC, F), H ** -0.5, 0.0625, ((1, 4), (2, 4)))
    down_two = noise_with(key_of[6], (F, HB, HC), F ** -0.5, 0.09375, ((0, 4), (2, 4)), (0, 1, 4, 2.0))
    return dict(tokens=tokens, gate_one=gate_one, up_one=up_one, down_one=down_one, gate_two=gate_two, up_two=up_two, down_two=down_two)


def split_rows(left, right, blocks):
    rows = left.shape[0]
    depth = left.shape[1]
    left_blocks = left.reshape(rows, blocks, depth // blocks).transpose(1, 0, 2)
    right_blocks = right.reshape(blocks, depth // blocks, right.shape[1])
    return left_blocks, right_blocks


def summed(left_blocks, right_blocks):
    start = jnp.zeros((left_blocks.shape[1], right_blocks.shape[2]), jnp.float32)

    def step(total, pair):
        term = jnp.dot(pair[0], pair[1], preferred_element_type=jnp.float32)
        term = lax.optimization_barrier(term.astype(jnp.bfloat16)).astype(jnp.float32)
        return total + term, None

    total, unused = lax.scan(step, start, (left_blocks, right_blocks))
    return total


def reference(tokens, gate_one, up_one, down_one, gate_two, up_two, down_two):
    rows = tokens.shape[0]
    left_blocks, gate_blocks = split_rows(tokens, gate_one, N_NARROW)
    unused, up_blocks = split_rows(tokens, up_one, N_NARROW)
    gate_first = summed(left_blocks, gate_blocks)
    up_first = summed(left_blocks, up_blocks)
    hidden_first = (jax.nn.silu(gate_first) * up_first).astype(jnp.bfloat16)
    hidden_blocks, down_blocks = split_rows(hidden_first, down_one, N_WIDE)
    mixed_first = summed(hidden_blocks, down_blocks)
    middle = (tokens.astype(jnp.float32) + mixed_first).astype(jnp.bfloat16)

    inner = HC // N_WIDE
    middle_blocks = middle.reshape(rows, HB, N_WIDE, inner).transpose(2, 0, 1, 3).reshape(N_WIDE, rows, HB * inner)
    gate_second_blocks = gate_two.reshape(HB, N_WIDE, inner, F).transpose(1, 0, 2, 3).reshape(N_WIDE, HB * inner, F)
    up_second_blocks = up_two.reshape(HB, N_WIDE, inner, F).transpose(1, 0, 2, 3).reshape(N_WIDE, HB * inner, F)
    gate_second = summed(middle_blocks, gate_second_blocks)
    up_second = summed(middle_blocks, up_second_blocks)
    hidden_second = (jax.nn.silu(gate_second) * up_second).astype(jnp.bfloat16)
    hidden_blocks2, down_blocks2 = split_rows(hidden_second, down_two.reshape(F, H), N_NARROW)
    mixed_second = summed(hidden_blocks2, down_blocks2)
    return (middle.astype(jnp.float32) + mixed_second).astype(jnp.bfloat16)
```

```python
import functools

import jax
import jax.numpy as jnp
from jax import lax
from jax.experimental import pallas as pl
from jax.experimental.pallas import tpu as pltpu
from jax.sharding import PartitionSpec as P

BF = jnp.bfloat16
F32 = jnp.float32
LINE = 4
MIB = 1024 * 1024
LAG = 2


def swiglu(gate, up_value):
    return (jax.nn.silu(gate) * up_value).astype(BF)


def plain(tokens, gate_one, up_one, down_one, gate_two, up_two, down_two):
    def layer(entries, gate, up, down, gather, scatter):
        whole = lax.all_gather(entries, gather, axis=1, tiled=True)
        shares = [
            lax.psum_scatter(
                jnp.dot(whole, w, preferred_element_type=F32).astype(BF),
                scatter, scatter_dimension=1, tiled=True,
            ).astype(F32)
            for w in (gate, up)
        ]
        hidden = lax.all_gather(swiglu(*shares), scatter, axis=1, tiled=True)
        part = jnp.dot(hidden, down, preferred_element_type=F32).astype(BF)
        mixed = lax.psum_scatter(part, gather, scatter_dimension=1, tiled=True)
        return (entries.astype(F32) + mixed.astype(F32)).astype(BF)

    middle = layer(tokens, gate_one, up_one, down_one, "wide", "narrow")
    return layer(
        middle,
        gate_two.reshape(-1, gate_two.shape[2]),
        up_two.reshape(-1, up_two.shape[2]),
        down_two.reshape(down_two.shape[0], -1),
        "narrow", "wide",
    )


def kernel(
    tok, g1, u1, d1, g2, u2, d2, out,
    wgu, wd, tokens, part, near, across, hid1, dpart, zr, zl, mid, yr, yl, hid2,
    near8, across8, acc_gu, acc_h, wsem, tsem, send_sems, recv_sems,
):
    z = lax.axis_index("wide")
    n = lax.axis_index("narrow")
    core = lax.rem(n, 2)
    chip = n // 2
    twin = chip * 2 + (1 - core)
    peer = (1 - chip) * 2 + core
    far = (1 - chip) * 2 + (1 - core)
    halves, rows = tokens.shape[0], tokens.shape[2]
    quarter = rows // LINE
    depth = tokens.shape[3]
    units = hid1.shape[2]

    def load(slot, src, dst):
        copy = pltpu.make_async_copy(src, dst, wsem.at[slot])
        copy.start()
        return copy

    own_rows = [
        pltpu.make_async_copy(tok.at[pl.ds(m * rows, rows)], tokens.at[m, z], tsem.at[m])
        for m in range(halves)
    ]
    for copy in own_rows:
        copy.start()
    loads = {
        "gu1": [load(0, g1, wgu.at[0]), load(1, u1, wgu.at[1])],
        "d1": [load(2, d1, wd)],
    }

    barrier = pltpu.get_barrier_semaphore()
    pl.semaphore_signal(barrier, inc=1, device_id={"narrow": twin})
    pl.semaphore_signal(barrier, inc=1, device_id={"narrow": peer})

    @pl.when(z > 0)
    def _():
        pl.semaphore_signal(barrier, inc=1, device_id={"wide": z - 1})

    @pl.when(z < LINE - 1)
    def _():
        pl.semaphore_signal(barrier, inc=1, device_id={"wide": z + 1})

    inner = jnp.logical_and(z > 0, z < LINE - 1)

    @pl.when(inner)
    def _():
        pl.semaphore_wait(barrier, 4)

    @pl.when(jnp.logical_not(inner))
    def _():
        pl.semaphore_wait(barrier, 3)

    counter = [0]

    def message(src, dst, device):
        i = counter[0]
        counter[0] += 1
        return pltpu.make_async_remote_copy(
            src_ref=src, dst_ref=dst, send_sem=send_sems.at[i], recv_sem=recv_sems.at[i],
            device_id=device, device_id_type=pl.DeviceIdType.MESH,
        )

    pending = [[] for _ in range(halves)]

    def guarded(cond, f):
        if cond is None:
            f()
        else:
            pl.when(cond)(f)

    def start(m, copy, cond=None):
        guarded(cond, copy.start)
        pending[m].append((cond, copy.wait_send))

    def arrive(copy, cond=None):
        guarded(cond, copy.wait_recv)

    def flush(m):
        for cond, wait in pending[m]:
            guarded(cond, wait)
        pending[m].clear()

    def piece(i):
        return pl.ds(pl.multiple_of(i * quarter, quarter), quarter)

    right, left = {"wide": z + 1}, {"wide": z - 1}

    def gather_line(m, at):
        previous = None
        for step in range(1, LINE):
            if previous is not None:
                yield
                arrive(previous[0], z >= step - 1)
                arrive(previous[1], z <= LINE - step)
            own = step - 1
            to_right = message(at(lax.max(z - own, 0)), at(lax.max(z - own, 0)), right)
            to_left = message(at(lax.min(z + own, LINE - 1)), at(lax.min(z + own, LINE - 1)), left)
            start(m, to_right, jnp.logical_and(z >= own, z < LINE - 1))
            start(m, to_left, jnp.logical_and(z + own < LINE, z > 0))
            previous = (to_right, to_left)
        yield
        arrive(previous[0], z >= LINE - 1)
        arrive(previous[1], z <= 0)

    def scatter_line(m, at, from_left, from_right):
        back = LINE - 1 - z
        previous = None

        def add(index, ref, slot):
            dst = at(index)
            dst[...] = (dst[...].astype(F32) + ref[slot].astype(F32)).astype(BF)

        for step in range(1, LINE):
            goes_right = jnp.logical_and(z <= step - 1, z < LINE - 1)
            goes_left = jnp.logical_and(back <= step - 1, back < LINE - 1)
            to_r = lax.min(z + LINE - step, LINE - 1)
            to_l = LINE - 1 - lax.min(back + LINE - step, LINE - 1)
            if previous is not None:
                yield
                arrive(previous[0], jnp.logical_and(z >= 1, z <= step - 1))
                arrive(previous[1], jnp.logical_and(back >= 1, back <= step - 1))

                @pl.when(jnp.logical_and(goes_right, z >= 1))
                def _():
                    add(to_r, from_left, step - 2)

            to_right = message(at(to_r), from_left.at[step - 1], right)
            start(m, to_right, goes_right)
            if previous is not None:
                @pl.when(jnp.logical_and(goes_left, back >= 1))
                def _():
                    add(to_l, from_right, step - 2)

            to_left = message(at(to_l), from_right.at[step - 1], left)
            start(m, to_left, goes_left)
            previous = (to_right, to_left)
        yield
        arrive(previous[0], z >= 1)
        arrive(previous[1], back >= 1)

    def gather_narrow(m, at):
        a = message(at(n), at(n), {"narrow": peer})
        b = message(at(n), at(n), {"narrow": twin})
        start(m, a)
        start(m, b)
        yield
        arrive(a)
        c = message(at(peer), at(peer), {"narrow": twin})
        start(m, c)
        yield
        arrive(b)
        arrive(c)

    def scatter_narrow(m, at, two, one):
        copies = []
        for i in range(2):
            copies.append(message(at(i * 2 + (1 - core)), two.at[i], {"narrow": twin}))
            start(m, copies[-1])
        yield
        for copy in copies:
            arrive(copy)
        dst = at(peer)
        dst[...] = (dst[...].astype(F32) + two[1 - chip].astype(F32)).astype(BF)
        over = message(at(peer), one, {"narrow": peer})
        start(m, over)
        yield
        arrive(over)

    def gate_up(m, src):
        tile = 256

        def body(i, carry):
            c = pl.ds(pl.multiple_of(i * tile, tile), tile)
            for w in range(2):
                total = jnp.dot(src[m, 0], wgu[w, 0:depth, c], preferred_element_type=F32)
                for s in range(1, LINE):
                    total += jnp.dot(
                        src[m, s], wgu[w, s * depth:(s + 1) * depth, c], preferred_element_type=F32
                    )
                dst = pl.ds(pl.multiple_of(w * units + i * tile, tile), tile)
                part[m, :, dst] = total.astype(BF)
            return carry

        lax.fori_loop(0, units // tile, body, 0)

    def down(m, hidden):
        for g in range(2):
            total = jnp.dot(
                hidden[m], wd[:, g * 2 * depth:(g + 1) * 2 * depth], preferred_element_type=F32
            )
            dpart[m, 2 * g] = total[:, :depth].astype(BF)
            dpart[m, 2 * g + 1] = total[:, depth:].astype(BF)

    def activate(g, u):
        return (g / (1.0 + jnp.exp(-g)) * u).astype(BF)

    def pipeline(m):
        last = m == halves - 1
        own_rows[m].wait()
        yield from gather_line(m, lambda i: tokens.at[m, i])
        if m == 0:
            for copy in loads["gu1"]:
                copy.wait()
        gate_up(m, tokens)
        at = lambda i: part.at[m, piece(i)]
        yield from scatter_narrow(m, at, near.at[m], across.at[m])
        if last:
            loads["gu2"] = [load(0, g2, wgu.at[0]), load(1, u2, wgu.at[1])]
        g, u = (
            part[m, piece(n), s].astype(F32)
            + near[m, chip, :, s].astype(F32)
            + across[m, :, s].astype(F32)
            for s in (slice(0, units), slice(units, 2 * units))
        )
        hid1[m, piece(n)] = activate(g, u)
        yield from gather_narrow(m, lambda i: hid1.at[m, piece(i)])
        if m == 0:
            loads["d1"][0].wait()
        down(m, hid1)
        if last:
            loads["d2"] = [load(2, d2, wd)]
        yield from scatter_line(m, lambda i: dpart.at[m, i], zr.at[m], zl.at[m])
        acc_h[...] = tokens[m, z].astype(F32) + dpart[m, z].astype(F32)

        @pl.when(z >= 1)
        def _():
            acc_h[...] += zr[m, LINE - 2].astype(F32)

        @pl.when(z < LINE - 1)
        def _():
            acc_h[...] += zl[m, LINE - 2].astype(F32)

        mid[m, n] = acc_h[...].astype(BF)
        yield from gather_narrow(m, lambda i: mid.at[m, i])
        if m == 0:
            for copy in loads["gu2"]:
                copy.wait()
        flush(m)
        gate_up(m, mid)
        yield from scatter_line(m, at, yr.at[m], yl.at[m])
        acc_gu[...] = part[m, piece(z)].astype(F32)

        @pl.when(z >= 1)
        def _():
            acc_gu[...] += yr[m, LINE - 2].astype(F32)

        @pl.when(z < LINE - 1)
        def _():
            acc_gu[...] += yl[m, LINE - 2].astype(F32)

        hid2[m, piece(z)] = activate(acc_gu[:, :units], acc_gu[:, units:])
        yield from gather_line(m, lambda i: hid2.at[m, piece(i)])
        if m == 0:
            loads["d2"][0].wait()
        down(m, hid2)
        yield from scatter_narrow(m, lambda i: dpart.at[m, i], near8.at[m], across8.at[m])
        out[pl.ds(m * rows, rows)] = (
            mid[m, n].astype(F32) + dpart[m, n].astype(F32)
            + near8[m, chip].astype(F32) + across8[m].astype(F32)
        ).astype(BF)
        flush(m)

    runs = [pipeline(m) for m in range(halves)]
    alive = [True] * halves
    turn = 0
    while any(alive):
        for m in range(halves):
            if alive[m] and turn >= m * LAG:
                try:
                    next(runs[m])
                except StopIteration:
                    alive[m] = False
        turn += 1


N_MESSAGES = 2 * 36


def fused(tokens, gate_one, up_one, down_one, gate_two, up_two, down_two):
    m, rows, depth = 2, tokens.shape[0] // 2, tokens.shape[1]
    width, units = gate_one.shape
    quarter = rows // LINE
    vmem = pltpu.VMEM
    scratch = [
        vmem((2, width, units), BF),
        vmem((units, width), BF),
        vmem((m, LINE, rows, depth), BF),
        vmem((m, rows, 2 * units), BF),
        vmem((m, 2, quarter, 2 * units), BF),
        vmem((m, quarter, 2 * units), BF),
        vmem((m, rows, units), BF),
        vmem((m, LINE, rows, depth), BF),
        vmem((m, LINE - 1, rows, depth), BF),
        vmem((m, LINE - 1, rows, depth), BF),
        vmem((m, LINE, rows, depth), BF),
        vmem((m, LINE - 1, quarter, 2 * units), BF),
        vmem((m, LINE - 1, quarter, 2 * units), BF),
        vmem((m, rows, units), BF),
        vmem((m, 2, rows, depth), BF),
        vmem((m, rows, depth), BF),
        vmem((quarter, 2 * units), F32),
        vmem((rows, depth), F32),
        pltpu.SemaphoreType.DMA((3,)),
        pltpu.SemaphoreType.DMA((2,)),
        pltpu.SemaphoreType.DMA((N_MESSAGES,)),
        pltpu.SemaphoreType.DMA((N_MESSAGES,)),
    ]
    flops = 2 * tokens.shape[0] * width * units * 6
    return pl.pallas_call(
        kernel,
        out_shape=jax.ShapeDtypeStruct(tokens.shape, BF),
        in_specs=[pl.BlockSpec(memory_space=pl.ANY)] * 7,
        out_specs=pl.BlockSpec(memory_space=pltpu.VMEM),
        scratch_shapes=scratch,
        compiler_params=pltpu.CompilerParams(
            collective_id=0, has_side_effects=True, vmem_limit_bytes=60 * MIB
        ),
        cost_estimate=pl.CostEstimate(
            flops=flops, bytes_accessed=12 * width * units, transcendentals=0
        ),
    )(
        tokens, gate_one, up_one, down_one,
        gate_two.reshape(-1, gate_two.shape[2]),
        up_two.reshape(-1, up_two.shape[2]),
        down_two.reshape(down_two.shape[0], -1),
    )


def fits(mesh, tokens, gate_one, up_one, down_one, gate_two, up_two, down_two):
    rows, depth = tokens.shape
    width, units = gate_one.shape
    return (
        mesh.shape["wide"] == LINE and mesh.shape["narrow"] == LINE
        and rows % (32 * LINE) == 0 and units % 256 == 0 and depth % 64 == 0
        and width == LINE * depth and gate_two.shape[:2] == (LINE, depth)
        and 12 * width * units < 50 * MIB
    )


def solution(mesh):
    def per_device(*arrays):
        return (fused if fits(mesh, *arrays) else plain)(*arrays)

    return jax.shard_map(
        per_device,
        mesh=mesh,
        in_specs=(
            P("groups", ("narrow", "wide")),
            P("narrow", "wide"),
            P("narrow", "wide"),
            P("wide", "narrow"),
            P(None, "wide", "narrow"),
            P(None, "wide", "narrow"),
            P("narrow", None, "wide"),
        ),
        out_specs=P("groups", ("narrow", "wide")),
        check_vma=False,
    )
```
